256 devices in a mesh: dp: 8 (over y_lo, x), expert: 32 (over z, y_hi, core).
Axes of the slice: x: 4, y: 4 (y_hi: 2, y_lo: 2; y = y_hi * 2 + y_lo), z: 8, core: 2. Of those that a mesh axis runs over, the one named last changes fastest.
Arguments:
- hidden: bfloat16 [12288, 8, 768], P('expert'), may hold values from -6 to 6
- expert_ids: int32 [12288, 8], P('expert'), may hold values from 0 to 63, all different within a row; in each aligned block of 384 rows (0 to 383, 384 to 767, ...) at most 96 rows name the same one
- route_gates: float32 [12288, 8], P('expert'), may hold values from 0.05 to 0.45
- down_weight: bfloat16 [64, 768, 2048], P('expert', None, 'dp'), may hold values from -0.21875 to 0.21875
Outputs:
- mixed: bfloat16 [12288, 2048], P('expert')
The draws below stay inside these ranges and needn't reach their ends.
Inputs may be any that keep to these rules, and one draw needn't show every extreme that they name: `expert_ids`: each row names 8 different experts. Among the 384 tokens of one device (aligned blocks of 384 rows) no expert is named by more than 96 rows, and in at least one block some expert is named by exactly 96 rows.
All inputs are finite; a program needn't handle non-finite values.
Results may differ from the reference program's by a relative error of at most 0.0049.
Values may be sent and summed in bfloat16 or wider, within the bound.
A program may use at most 64 MiB of HBM per device.

```python
import math
import jax
import jax.numpy as jnp
import numpy as np
from jax import lax

D = 2048
FF = 768
TOP = 8
TOK_DEV = 384
EXPERTS = 64
TOKENS = 12288
CAPACITY = 96
N_EXPERT = 32


def level_of(own_key, shape, cuts, least, largest):
    factor_of, own = 1.0, jax.random.fold_in(own_key, 6)
    for dim, blocks in cuts:
        heights = jnp.exp(jax.random.uniform(jax.random.fold_in(own, dim), (blocks,), jnp.float32, least / len(cuts), largest / len(cuts)))
        factor_of = factor_of * jnp.repeat(heights, shape[dim] // blocks).reshape([-1 if axis == dim else 1 for axis in range(len(shape))])
    return factor_of


def assign_block(rng, own, number, rows, number_of, top, most, lean):
    ranking = jax.random.permutation(rng, number_of)
    crowded, usual = portions_of(number_of, rows * top, most, lean, True), portions_of(number_of, rows * top, most, lean, False)
    places = jnp.arange(number_of)

    def named(lengths, turn):
        used = int((lengths > 0).sum())
        fixed = max(1, used // 4)
        passed = fixed + (places - fixed + turn * (used - fixed)) % max(1, number_of - fixed)
        return jnp.zeros((number_of,), jnp.int32).at[ranking[jnp.where(places < fixed, places, passed)]].set(jnp.asarray(lengths, jnp.int32))

    lengths = jnp.where(number % 4 == 0, named(crowded, number // 4), named(usual, number - number // 4 - 1))
    mixed = jax.random.permutation(jax.random.fold_in(own, 3), number_of)
    source_of, taker = mixed[0:number_of // 2 * 2:2], mixed[1:number_of // 2 * 2:2]
    room = jnp.minimum(lengths[source_of] - 1, most - lengths[taker]) // 2
    room = jnp.where((source_of == ranking[0]) | (taker == ranking[0]) | (lengths[taker] == 0), 0, jnp.maximum(room, 0))
    passed = jax.random.randint(jax.random.fold_in(own, 4), (number_of // 2,), 0, 1 << 20) % (room + 1)
    lengths = lengths.at[source_of].add(-passed).at[taker].add(passed)
    labels = jnp.searchsorted(jnp.cumsum(lengths), jnp.arange(rows * top), side="right").astype(jnp.int32)
    listing = labels.reshape(top, rows).T
    listing = listing[jax.random.permutation(jax.random.fold_in(own, 1), rows)]
    turn = jax.random.randint(jax.random.fold_in(own, 2), (rows, 1), 0, top)
    return jnp.take_along_axis(listing, (jnp.arange(top)[None, :] + turn) % top, axis=1)


def portions_of(amount, total, reach, skew, full):
    portions = [(1 << 20) // math.isqrt(standing ** skew) + 1 for standing in range(1, amount + 1)]
    largest = reach if full else min(reach, max(-(-total // amount), total * portions[0] // sum(portions)))
    least = 1 if total - largest >= amount - 1 else 0
    counts, surplus = [largest] + [least] * (amount - 1), total - largest - least * (amount - 1)
    while surplus > 0:
        free = [i for i in range(1, amount) if counts[i] < largest] or [i for i in range(1, amount) if counts[i] < reach]
        whole, left = sum([portions[i] for i in free]), surplus
        for i in free:
            more = min(reach - counts[i], max(1, left * portions[i] // whole), surplus)
            counts[i] = counts[i] + more
            surplus = surplus - more
    return np.array(counts)


def scatter_about(stream_key, shape, deviation, most, cuts=(), kind=jnp.bfloat16):
    drawn = jax.random.normal(stream_key, shape, jnp.float32) * deviation
    if len(cuts) > 0:
        drawn = level_of(stream_key, shape, cuts, -0.22, 0.18) * drawn
    return jnp.clip(drawn, min=-most, max=most).astype(kind)


def setup_inputs(seed: int = 0) -> dict:
    key_list = jax.random.split(jax.random.key(seed), 5)
    hidden = scatter_about(key_list[0], (TOKENS, TOP, FF), 1.0, 6.0, ((0, 32),))
    expert_ids_keys = jax.random.split(jax.random.fold_in(key_list[1], 1), TOKENS // TOK_DEV)
    expert_ids_turns = jax.random.permutation(jax.random.fold_in(key_list[1], 3), TOKENS // TOK_DEV)
    expert_ids = jax.vmap(lambda own, number: assign_block(jax.random.fold_in(key_list[1], 2), own, number, TOK_DEV, EXPERTS, TOP, CAPACITY, 2))(expert_ids_keys, expert_ids_turns).reshape((TOKENS, TOP))
    route_gates = jnp.clip(0.05 + 0.39999999 * jax.random.uniform(key_list[2], (TOKENS, TOP), jnp.float32) ** level_of(key_list[2], (TOKENS, TOP), ((0, 32),), -0.2, 0.2), 0.05, 0.45)
    down_weight = scatter_about(key_list[3], (EXPERTS, FF, D), FF ** -0.5, 0.21875, ((0, 32), (2, 8)))
    return dict(hidden=hidden, expert_ids=expert_ids, route_gates=route_gates, down_weight=down_weight)


def block_output(block_ids, block_gates, block_hidden, down_wide):
    route_total = TOK_DEV * TOP
    flat_ids = block_ids.reshape(route_total).astype(jnp.int32)
    expert_range = jnp.arange(EXPERTS, dtype=jnp.int32)
    onehot = (flat_ids[:, None] == expert_range[None, :]).astype(jnp.int32)
    earlier = jnp.cumsum(onehot, axis=0) - onehot
    position = jnp.sum(earlier * onehot, axis=1).astype(jnp.int32)
    slot_index = (flat_ids * CAPACITY + position).astype(jnp.int32)
    route_range = jnp.arange(route_total, dtype=jnp.int32)
    slot_table = jnp.full((EXPERTS * CAPACITY,), route_total, jnp.int32).at[slot_index].set(route_range)
    row_table = jnp.concatenate([block_hidden.reshape(route_total, FF), jnp.zeros((1, FF), block_hidden.dtype)], axis=0)
    gathered = row_table[slot_table].reshape(EXPERTS, CAPACITY, FF).astype(jnp.float32)
    product = jnp.einsum("ecf,efd->ecd", gathered, down_wide).astype(jnp.bfloat16)
    per_route = product.reshape(EXPERTS * CAPACITY, D)[slot_index].astype(jnp.float32)
    weighted = per_route.reshape(TOK_DEV, TOP, D) * block_gates[:, :, None]
    return jnp.sum(weighted, axis=1).astype(jnp.bfloat16)


def reference(hidden, expert_ids, route_gates, down_weight):
    down_wide = down_weight.astype(jnp.float32)
    blocks = (expert_ids.reshape(N_EXPERT, TOK_DEV, TOP), route_gates.reshape(N_EXPERT, TOK_DEV, TOP), hidden.reshape(N_EXPERT, TOK_DEV, TOP, FF))
    outputs = lax.map(lambda pieces: block_output(pieces[0], pieces[1], pieces[2], down_wide), blocks)
    return outputs.reshape(TOKENS, D)
```

```python
import functools

import jax
import jax.numpy as jnp
from jax import lax
from jax.experimental import pallas as pl
from jax.experimental.pallas import tpu as pltpu
from jax.sharding import PartitionSpec as P

MESH = pl.DeviceIdType.MESH
TOKENS = 384
TOP = 8
FF = 768
COLS = 256
BLOCK = 32
BLOCKS = TOKENS // BLOCK
ROUTES = BLOCK * TOP
HOPS = 7
SUBS = 6
SUB_ROWS = TOKENS * TOP // 4 // SUBS
OWN_BATCH = 16


def pick_rows(meta, hidden, picked, block, experts):
    ids = meta[pl.ds(block, 1), :]
    gates = meta[pl.ds(BLOCKS + block, 1), :]
    shape = (BLOCK, ROUTES)
    owner = lax.broadcasted_iota(jnp.int32, shape, 1) // TOP
    mine = owner == lax.broadcasted_iota(jnp.int32, shape, 0)
    names = jnp.where(mine, jnp.broadcast_to(ids, shape), -1.0)
    chosen = jnp.concatenate(
        [jnp.where(names == e, 1.0, 0.0).astype(jnp.bfloat16) for e in experts], axis=0
    )
    square = (ROUTES, ROUTES)
    diagonal = lax.broadcasted_iota(jnp.int32, square, 0) == lax.broadcasted_iota(
        jnp.int32, square, 1
    )
    column = jnp.sum(
        jnp.where(diagonal, jnp.broadcast_to(gates, square), 0.0), axis=1, keepdims=True
    )
    rows = hidden[pl.ds(pl.multiple_of(block * ROUTES, ROUTES), ROUTES), :]
    rows = (rows.astype(jnp.float32) * column).astype(jnp.bfloat16)
    result = jnp.dot(chosen, rows, preferred_element_type=jnp.float32).astype(jnp.bfloat16)
    for i in range(len(experts)):
        picked[pl.ds(pl.multiple_of(block * BLOCK, BLOCK), BLOCK), i * FF : (i + 1) * FF] = result[
            i * BLOCK : (i + 1) * BLOCK
        ]


def kernel(
    meta,
    hidden_in,
    weights_in,
    out,
    held,
    hidden,
    hidden_far,
    meta_far,
    picked,
    picked_far,
    total,
    total_far,
    sent,
    came,
    gathered,
    ring_send,
    ring_recv,
    core_send,
    core_recv,
    rows_send,
    rows_recv,
    end_send,
    end_recv,
    near_sem,
    out_sem,
):
    dp = lax.axis_index("dp")
    ex = lax.axis_index("expert")
    x, y_lo = lax.rem(dp, 4), dp // 4
    z, y_hi, core = ex // 4, lax.rem(ex // 2, 2), lax.rem(ex, 2)

    def device(x_, y_lo_, z_, y_hi_, core_):
        return (y_lo_ * 4 + lax.rem(x_ + 4, 4), lax.rem(z_ + 8, 8) * 4 + y_hi_ * 2 + core_)

    up, down = device(x, y_lo, z + 1, y_hi, core), device(x, y_lo, z - 1, y_hi, core)
    sibling = device(x, y_lo, z, y_hi, 1 - core)
    across = device(x, 1 - y_lo, z, 1 - y_hi, core)
    beside = device(x, 1 - y_lo, z, y_hi, core)
    right, left = device(x + 1, y_lo, z, y_hi, core), device(x - 1, y_lo, z, y_hi, core)
    opposite = device(x, y_lo, z, 1 - y_hi, core)

    def remote(src, dst, send_sem, recv_sem, to):
        return pltpu.make_async_remote_copy(
            src_ref=src,
            dst_ref=dst,
            send_sem=send_sem,
            recv_sem=recv_sem,
            device_id=to,
            device_id_type=MESH,
        )

    def place(first, count=1):
        return held.at[pl.ds(first * FF, count * FF)]

    def ring_copy(way, hop):
        if hop < 2:
            expert = hop if way == 0 else 1 - hop
            src = weights_in.at[pl.ds(expert * FF, FF)]
        else:
            src = place(4 * (hop - 1) + way)
        return remote(
            src,
            place(4 * (hop + 1) + way),
            ring_send.at[way, hop],
            ring_recv.at[way, hop],
            up if way == 0 else down,
        )

    def core_copy(group):
        src = weights_in if group == 0 else place(4 * group, 2)
        return remote(
            src, place(4 * group + 2, 2), core_send.at[group], core_recv.at[group], sibling
        )

    def experts_of(group):
        found = []
        for c in (core, 1 - core):
            for way in (0, 1):
                if group == 0:
                    where, which = z, way
                else:
                    hop = group - 1
                    step = 1 + hop // 2
                    where = lax.rem(z + (8 - step if way == 0 else step), 8)
                    which = hop % 2 if way == 0 else 1 - hop % 2
                found.append(((where * 2 + y_hi) * 2 + c) * 2 + which)
        return [e.astype(jnp.float32) for e in found]

    x_odd = lax.rem(x, 2)
    quarters = [
        x_odd * 2 + y_lo,
        x_odd * 2 + 1 - y_lo,
        (1 - x_odd) * 2 + y_lo,
        (1 - x_odd) * 2 + 1 - y_lo,
    ]

    def rows_of(quarter, sub):
        start = pl.multiple_of(quarter * (SUBS * SUB_ROWS) + sub * SUB_ROWS, SUB_ROWS)
        return pl.ds(start, SUB_ROWS)

    def rows_copy(kind, sub):
        quarter = quarters[(1, 0, 0, 1)[kind]]
        rows = rows_of(quarter, sub)
        src = (hidden_in if kind == 0 else hidden_far).at[rows]
        to = (across, beside, left, right)[kind]
        return remote(
            src, hidden_far.at[rows], rows_send.at[kind, sub], rows_recv.at[kind, sub], to
        )

    meta_copy = remote(meta, meta_far, end_send.at[0], end_recv.at[0], across)

    barrier = pltpu.get_barrier_semaphore()
    friends = (up, down, sibling, across, beside, right, left, opposite)
    for friend in friends:
        pl.semaphore_signal(barrier, inc=1, device_id=friend, device_id_type=MESH)
    near_hidden = pltpu.make_async_copy(hidden_in, hidden, near_sem.at[0])
    near_weights = pltpu.make_async_copy(weights_in, place(0, 2), near_sem.at[1])
    near_hidden.start()
    near_weights.start()
    pl.semaphore_wait(barrier, len(friends))

    for hop in (0, 1):
        for way in (0, 1):
            ring_copy(way, hop).start()
    meta_copy.start()
    for sub in range(SUBS):
        rows_copy(0, sub).start()
    core_copy(0).start()

    total[...] = jnp.zeros_like(total)
    total_far[...] = jnp.zeros_like(total_far)
    experts = [e for group in range(8) for e in experts_of(group)]

    def ring(hop):
        for way in (0, 1):
            ring_copy(way, hop).wait_recv()
            if hop + 2 < HOPS:
                ring_copy(way, hop + 2).start()
        core_copy(hop + 1).start()

    def from_across(sub):
        rows_copy(0, sub).wait_recv()
        rows_copy(1, sub).start()
        rows_copy(2, sub).start()

    def from_beside(sub):
        rows_copy(1, sub).wait_recv()
        rows_copy(3, sub).start()

    def pick_near(batch, first, count):
        @pl.loop(first, first + count)
        def _(block):
            pick_rows(
                meta, hidden, picked, block, experts[batch * OWN_BATCH : (batch + 1) * OWN_BATCH]
            )

    def pick_far(kind):
        @pl.loop(0, BLOCKS // 4)
        def _(i):
            pick_rows(
                meta_far, hidden_far, picked_far, quarters[kind] * (BLOCKS // 4) + i, experts
            )

    def multiply(acc, rows, column_group, group):
        acc[...] += jnp.dot(
            rows[:, column_group * 4 * FF : (column_group + 1) * 4 * FF],
            held[group * 4 * FF : (group + 1) * 4 * FF, :],
            preferred_element_type=jnp.float32,
        )

    def multiply_near(group):
        multiply(total, picked, group % 4, group)

    def multiply_far(group):
        multiply(total_far, picked_far, group, group)

    near_hidden.wait()
    pick_near(0, 0, 6)
    from_across(0)
    pick_near(0, 6, 6)
    from_across(1)
    ring(0)
    from_beside(0)
    near_weights.wait()
    core_copy(0).wait_recv()
    multiply_near(0)
    core_copy(1).wait_recv()
    multiply_near(1)
    from_across(2)
    from_beside(1)
    from_across(3)
    ring(1)
    from_beside(2)
    core_copy(2).wait_recv()
    multiply_near(2)
    from_across(4)
    from_beside(3)
    ring(2)
    from_across(5)
    core_copy(3).wait_recv()
    multiply_near(3)
    from_beside(4)
    pick_near(1, 0, 6)
    from_beside(5)
    pick_near(1, 6, 6)
    meta_copy.wait_recv()
    pick_far(0)
    pick_far(1)
    ring(3)
    for sub in range(SUBS):
        rows_copy(2, sub).wait_recv()
    pick_far(2)
    for sub in range(SUBS):
        rows_copy(3, sub).wait_recv()
    pick_far(3)
    core_copy(4).wait_recv()
    multiply_near(4)
    multiply_far(0)
    multiply_far(1)
    ring(4)
    multiply_far(2)
    multiply_far(3)
    multiply_far(4)
    core_copy(5).wait_recv()
    multiply_near(5)
    multiply_far(5)
    ring(5)
    core_copy(6).wait_recv()
    multiply_near(6)
    multiply_far(6)
    ring(6)
    core_copy(7).wait_recv()
    multiply_far(7)

    sent[...] = total_far[...].astype(jnp.bfloat16)
    sums = remote(sent, came, end_send.at[1], end_recv.at[1], opposite)
    sums.start()
    multiply_near(7)
    sums.wait_recv()
    gathered[dp] = (total[...] + came[...].astype(jnp.float32)).astype(jnp.bfloat16)

    half = TOKENS // 2
    dp_of = lambda x_, y_lo_: y_lo_ * 4 + lax.rem(x_ + 4, 4)

    def hand_on(number, block, to, rows=None):
        ref = gathered.at[block] if rows is None else gathered.at[block, pl.ds(rows, half)]
        return remote(ref, ref, end_send.at[number], end_recv.at[number], to)

    def write(number, block):
        return pltpu.make_async_copy(
            gathered.at[block],
            out.at[:, pl.ds(pl.multiple_of(block * COLS, COLS), COLS)],
            out_sem.at[number],
        )

    other = 1 - y_lo
    mine_up = hand_on(2, dp, beside)
    mine_right, mine_left = hand_on(3, dp, right), hand_on(4, dp, left)
    mine_right.start()
    mine_left.start()
    mine_up.start()
    write(0, dp).start()
    from_left, from_right = dp_of(x - 1, y_lo), dp_of(x + 1, y_lo)
    far_right, far_left = hand_on(5, from_left, right, 0), hand_on(6, from_right, left, half)
    mine_right.wait_recv()
    far_right.start()
    write(1, from_left).start()
    mine_left.wait_recv()
    far_left.start()
    write(2, from_right).start()
    mine_up.wait_recv()
    twin = dp_of(x, other)
    twin_right, twin_left = hand_on(7, twin, right), hand_on(8, twin, left)
    twin_right.start()
    twin_left.start()
    write(3, twin).start()
    far_right.wait_recv()
    far_left.wait_recv()
    far = dp_of(x + 2, y_lo)
    far_up = hand_on(9, far, beside)
    far_up.start()
    write(4, far).start()
    twin_right.wait_recv()
    write(5, dp_of(x - 1, other)).start()
    twin_left.wait_recv()
    write(6, dp_of(x + 1, other)).start()
    far_up.wait_recv()
    write(7, dp_of(x + 2, other)).start()

    for way in (0, 1):
        for hop in range(HOPS):
            ring_copy(way, hop).wait_send()
    for group in range(8):
        core_copy(group).wait_send()
    for kind in range(4):
        for sub in range(SUBS):
            rows_copy(kind, sub).wait_send()
    for copy in (
        meta_copy,
        sums,
        mine_up,
        mine_right,
        mine_left,
        far_right,
        far_left,
        twin_right,
        twin_left,
        far_up,
    ):
        copy.wait_send()
    blocks = (
        dp,
        from_left,
        from_right,
        twin,
        far,
        dp_of(x - 1, other),
        dp_of(x + 1, other),
        dp_of(x + 2, other),
    )
    for number, block in enumerate(blocks):
        write(number, block).wait()


def local(hidden, expert_ids, route_gates, down_weight):
    routes = TOKENS * TOP
    meta = jnp.concatenate(
        [
            expert_ids.astype(jnp.float32).reshape(BLOCKS, ROUTES),
            route_gates.reshape(BLOCKS, ROUTES),
        ],
        axis=0,
    )
    anywhere = pl.BlockSpec(memory_space=pl.ANY)
    dma = pltpu.SemaphoreType.DMA
    return pl.pallas_call(
        kernel,
        out_shape=jax.ShapeDtypeStruct((TOKENS, 8 * COLS), jnp.bfloat16),
        in_specs=[pl.BlockSpec(memory_space=pltpu.VMEM), anywhere, anywhere],
        out_specs=anywhere,
        scratch_shapes=[
            pltpu.VMEM((32 * FF, COLS), jnp.bfloat16),
            pltpu.VMEM((routes, FF), jnp.bfloat16),
            pltpu.VMEM((routes, FF), jnp.bfloat16),
            pltpu.VMEM((2 * BLOCKS, ROUTES), jnp.float32),
            pltpu.VMEM((TOKENS, OWN_BATCH * FF), jnp.bfloat16),
            pltpu.VMEM((TOKENS, 32 * FF), jnp.bfloat16),
            pltpu.VMEM((TOKENS, COLS), jnp.float32),
            pltpu.VMEM((TOKENS, COLS), jnp.float32),
            pltpu.VMEM((TOKENS, COLS), jnp.bfloat16),
            pltpu.VMEM((TOKENS, COLS), jnp.bfloat16),
            pltpu.VMEM((8, TOKENS, COLS), jnp.bfloat16),
            dma((2, HOPS)),
            dma((2, HOPS)),
            dma((8,)),
            dma((8,)),
            dma((4, SUBS)),
            dma((4, SUBS)),
            dma((10,)),
            dma((10,)),
            dma((2,)),
            dma((8,)),
        ],
        name="experts",
        compiler_params=pltpu.CompilerParams(
            collective_id=0, has_side_effects=True, vmem_limit_bytes=60 * 2**20
        ),
        cost_estimate=pl.CostEstimate(
            flops=2 * 2 * TOKENS * 32 * FF * COLS * 2,
            bytes_accessed=8 * 2**20,
            transcendentals=0,
        ),
    )(meta, hidden.reshape(routes, FF), down_weight.reshape(2 * FF, COLS))


def solution(mesh):
    placed = (
        P("expert", None, None),
        P("expert", None),
        P("expert", None),
        P("expert", None, "dp"),
    )
    return jax.shard_map(
        local, mesh=mesh, in_specs=placed, out_specs=P("expert", None), check_vma=False
    )
```

```python
import functools

import jax
import jax.numpy as jnp
from jax import lax
from jax.experimental import pallas as pl
from jax.experimental.pallas import tpu as pltpu
from jax.sharding import PartitionSpec as P

MESH = pl.DeviceIdType.MESH
TOKENS = 384
TOP = 8
FF = 768
COLS = 256
BLOCK = 32
BLOCKS = TOKENS // BLOCK
ROUTES = BLOCK * TOP
HOPS = 7
QUARTER = TOKENS * TOP // 4
PIECES = (128, 128, 128, 128, 128, 64, 64)
SUBS = len(PIECES)
OWN_BATCH = 16
WHOLE = 5
LATE = HOPS - WHOLE
HALF = COLS // 2
STEPS = WHOLE + 2 * LATE
PARTS = ((0, 0, TOKENS), (1, 0, TOKENS // 2), (1, TOKENS // 2, TOKENS // 2))


def pick_rows(meta, hidden, picked, block, experts):
    ids = meta[pl.ds(block, 1), :]
    gates = meta[pl.ds(BLOCKS + block, 1), :]
    shape = (BLOCK, ROUTES)
    owner = lax.broadcasted_iota(jnp.int32, shape, 1) // TOP
    mine = owner == lax.broadcasted_iota(jnp.int32, shape, 0)
    names = jnp.where(mine, jnp.broadcast_to(ids, shape), -1.0)
    chosen = jnp.concatenate(
        [jnp.where(names == e, 1.0, 0.0).astype(jnp.bfloat16) for e in experts], axis=0
    )
    square = (ROUTES, ROUTES)
    diagonal = lax.broadcasted_iota(jnp.int32, square, 0) == lax.broadcasted_iota(
        jnp.int32, square, 1
    )
    column = jnp.sum(
        jnp.where(diagonal, jnp.broadcast_to(gates, square), 0.0), axis=1, keepdims=True
    )
    rows = hidden[pl.ds(pl.multiple_of(block * ROUTES, ROUTES), ROUTES), :]
    rows = (rows.astype(jnp.float32) * column).astype(jnp.bfloat16)
    result = jnp.dot(chosen, rows, preferred_element_type=jnp.float32).astype(jnp.bfloat16)
    for i in range(len(experts)):
        picked[pl.ds(pl.multiple_of(block * BLOCK, BLOCK), BLOCK), i * FF : (i + 1) * FF] = result[
            i * BLOCK : (i + 1) * BLOCK
        ]


def lay_out(ids, gates, meta):
    wide = (128, ROUTES)
    spread = (
        lax.rem(lax.broadcasted_iota(jnp.int32, (TOP, ROUTES), 1), TOP)
        == lax.broadcasted_iota(jnp.int32, (TOP, ROUTES), 0)
    ).astype(jnp.float32)
    mine = lax.broadcasted_iota(jnp.int32, wide, 1) // TOP == lax.rem(
        lax.broadcasted_iota(jnp.int32, wide, 0), BLOCK
    )
    for chunk in range(TOKENS // 128):
        columns = slice(chunk * 128, (chunk + 1) * 128)
        for first, part in ((0, ids[:, columns].astype(jnp.float32)), (BLOCKS, gates[:, columns])):
            full = lax.dot_general(
                part,
                spread,
                (((0,), (0,)), ((), ())),
                precision=lax.Precision.HIGHEST,
                preferred_element_type=jnp.float32,
            )
            full = jnp.where(mine, full, 0.0)
            for i in range(128 // BLOCK):
                row = first + chunk * (128 // BLOCK) + i
                meta[row : row + 1, :] = jnp.sum(
                    full[i * BLOCK : (i + 1) * BLOCK], axis=0, keepdims=True
                )


def kernel(
    ids_in,
    gates_in,
    hidden_in,
    weights_in,
    out,
    meta,
    held,
    late,
    hidden,
    hidden_far,
    meta_far,
    picked,
    picked_far,
    total,
    total_far,
    sent,
    came,
    gathered,
    ring_send,
    ring_recv,
    core_send,
    core_recv,
    rows_send,
    rows_recv,
    end_send,
    end_recv,
    meta_sem,
    near_sem,
    out_sem,
):
    dp = lax.axis_index("dp")
    ex = lax.axis_index("expert")
    x, y_lo = lax.rem(dp, 4), dp // 4
    z, y_hi, core = ex // 4, lax.rem(ex // 2, 2), lax.rem(ex, 2)

    def device(x_, y_lo_, z_, y_hi_, core_):
        return (y_lo_ * 4 + lax.rem(x_ + 4, 4), lax.rem(z_ + 8, 8) * 4 + y_hi_ * 2 + core_)

    up, down = device(x, y_lo, z + 1, y_hi, core), device(x, y_lo, z - 1, y_hi, core)
    sibling = device(x, y_lo, z, y_hi, 1 - core)
    across = device(x, 1 - y_lo, z, 1 - y_hi, core)
    beside = device(x, 1 - y_lo, z, y_hi, core)
    right, left = device(x + 1, y_lo, z, y_hi, core), device(x - 1, y_lo, z, y_hi, core)
    opposite = device(x, y_lo, z, 1 - y_hi, core)
    farther = device(x + 2, y_lo, z, y_hi, core)

    def remote(src, dst, send_sem, recv_sem, to):
        return pltpu.make_async_remote_copy(
            src_ref=src,
            dst_ref=dst,
            send_sem=send_sem,
            recv_sem=recv_sem,
            device_id=to,
            device_id_type=MESH,
        )

    def place(group, first, count):
        return held.at[pl.ds((4 * group + first) * FF, count * FF)]

    def late_place(half, group, first, count):
        return late.at[half, pl.ds((4 * (group - WHOLE - 1) + first) * FF, count * FF)]

    def hop_of(step):
        if step < WHOLE:
            return step, None
        return WHOLE + (step - WHOLE) % LATE, (step - WHOLE) // LATE

    def ring_copy(way, step):
        hop, half = hop_of(step)
        if hop < 2:
            src = weights_in.at[pl.ds((hop if way == 0 else 1 - hop) * FF, FF)]
        elif hop - 2 < WHOLE:
            src = place(hop - 1, way, 1)
            if half is not None:
                src = held.at[pl.ds((4 * (hop - 1) + way) * FF, FF), pl.ds(half * HALF, HALF)]
        else:
            src = late_place(half, hop - 1, way, 1)
        dst = place(hop + 1, way, 1) if half is None else late_place(half, hop + 1, way, 1)
        return remote(
            src,
            dst,
            ring_send.at[way, step],
            ring_recv.at[way, step],
            up if way == 0 else down,
        )

    def core_copy(number):
        if number == 0:
            src, dst = weights_in, place(0, 2, 2)
        else:
            hop, half = hop_of(number - 1)
            if half is None:
                src, dst = place(hop + 1, 0, 2), place(hop + 1, 2, 2)
            else:
                src, dst = late_place(half, hop + 1, 0, 2), late_place(half, hop + 1, 2, 2)
        return remote(src, dst, core_send.at[number], core_recv.at[number], sibling)

    def experts_of(group):
        found = []
        for c in (core, 1 - core):
            for way in (0, 1):
                if group == 0:
                    where, which = z, way
                else:
                    hop = group - 1
                    step = 1 + hop // 2
                    where = lax.rem(z + (8 - step if way == 0 else step), 8)
                    which = hop % 2 if way == 0 else 1 - hop % 2
                found.append(((where * 2 + y_hi) * 2 + c) * 2 + which)
        return [e.astype(jnp.float32) for e in found]

    x_odd = lax.rem(x, 2)
    quarters = [
        x_odd * 2 + y_lo,
        x_odd * 2 + 1 - y_lo,
        (1 - x_odd) * 2 + y_lo,
        (1 - x_odd) * 2 + 1 - y_lo,
    ]

    def rows_of(quarter, sub):
        start = pl.multiple_of(quarter * QUARTER + sum(PIECES[:sub]), 64)
        return pl.ds(start, PIECES[sub])

    def rows_copy(kind, sub):
        quarter = quarters[(1, 0, 0, 1)[kind]]
        rows = rows_of(quarter, sub)
        src = (hidden_in if kind == 0 else hidden_far).at[rows]
        to = (across, beside, left, right)[kind]
        return remote(
            src, hidden_far.at[rows], rows_send.at[kind, sub], rows_recv.at[kind, sub], to
        )

    meta_copy = remote(meta, meta_far, meta_sem.at[0], meta_sem.at[1], across)

    barrier = pltpu.get_barrier_semaphore()
    friends = (up, down, sibling, across, beside, right, left, opposite, farther)
    for friend in friends:
        pl.semaphore_signal(barrier, inc=1, device_id=friend, device_id_type=MESH)
    near_hidden = pltpu.make_async_copy(hidden_in, hidden, near_sem.at[0])
    near_weights = pltpu.make_async_copy(weights_in, place(0, 0, 2), near_sem.at[1])
    near_hidden.start()
    near_weights.start()
    pl.semaphore_wait(barrier, len(friends))

    for hop in (0, 1):
        for way in (0, 1):
            ring_copy(way, hop).start()
    for sub in range(SUBS):
        rows_copy(0, sub).start()
    core_copy(0).start()
    lay_out(ids_in, gates_in, meta)
    meta_copy.start()

    total[...] = jnp.zeros_like(total)
    total_far[...] = jnp.zeros_like(total_far)
    experts = [e for group in range(8) for e in experts_of(group)]

    def ring(step):
        for way in (0, 1):
            ring_copy(way, step).wait_recv()
            if step + 2 < STEPS:
                ring_copy(way, step + 2).start()
        core_copy(step + 1).start()

    def from_across(sub):
        rows_copy(0, sub).wait_recv()
        rows_copy(1, sub).start()
        rows_copy(2, sub).start()

    def from_beside(sub):
        rows_copy(1, sub).wait_recv()
        rows_copy(3, sub).start()

    def pick_near(batch, first, count):
        @pl.loop(first, first + count)
        def _(block):
            pick_rows(
                meta, hidden, picked, block, experts[batch * OWN_BATCH : (batch + 1) * OWN_BATCH]
            )

    def pick_far(turn):
        for kind in (2, 3):
            for sub in range(2 * turn, 2 * turn + 2 + turn // 2):
                rows_copy(kind, sub).wait_recv()

        @pl.loop(0, 4)
        def _(kind):
            odd = x_odd + (kind // 2) * (1 - 2 * x_odd)
            low = y_lo + lax.rem(kind, 2) * (1 - 2 * y_lo)
            block = (odd * 2 + low) * (BLOCKS // 4) + turn
            pick_rows(meta_far, hidden_far, picked_far, block, experts)

    def multiply(acc, rows, column_group, group, half, first=0, count=4):
        left = rows[:, (column_group * 4 + first) * FF : (column_group * 4 + first + count) * FF]
        if half is None:
            start = (group * 4 + first) * FF
            acc[...] += jnp.dot(
                left, held[start : start + count * FF, :], preferred_element_type=jnp.float32
            )
        else:
            start = ((group - WHOLE - 1) * 4 + first) * FF
            acc[:, half * HALF : (half + 1) * HALF] += jnp.dot(
                left, late[half, start : start + count * FF, :], preferred_element_type=jnp.float32
            )

    def multiply_near(group, half=None, first=0, count=4):
        multiply(total, picked, group % 4, group, half, first, count)

    def multiply_far(group, half=None, first=0, count=4):
        multiply(total_far, picked_far, group, group, half, first, count)

    dp_of = lambda x_, y_lo_: y_lo_ * 4 + lax.rem(x_ + 4, 4)
    other = 1 - y_lo
    from_left, from_right, far = dp_of(x - 1, y_lo), dp_of(x + 1, y_lo), dp_of(x + 2, y_lo)
    twin = dp_of(x, other)
    blocks = (
        dp,
        from_left,
        from_right,
        twin,
        far,
        dp_of(x - 1, other),
        dp_of(x + 1, other),
        dp_of(x + 2, other),
    )

    def write(part, number):
        half, first, count = PARTS[part]
        block = blocks[number]
        start = pl.multiple_of(block * COLS + half * HALF, HALF)
        return pltpu.make_async_copy(
            gathered.at[half, block, pl.ds(first, count)],
            out.at[pl.ds(first, count), pl.ds(start, HALF)],
            out_sem.at[part, number],
        )

    def sums_copy(part):
        half, first, count = PARTS[part]
        rows = pl.ds(first, count)
        return remote(
            sent.at[half, rows],
            came.at[half, rows],
            end_send.at[part, 0],
            end_recv.at[part, 0],
            opposite,
        )

    gathers = {
        "mine_up": (1, dp, beside),
        "mine_far": (2, dp, farther),
        "mine_right": (3, dp, right),
        "mine_left": (4, dp, left),
        "twin_right": (5, twin, right),
        "twin_left": (6, twin, left),
        "far_up": (7, far, beside),
    }

    def gather(part, name):
        half, first, count = PARTS[part]
        number, block, to = gathers[name]
        ref = gathered.at[half, block, pl.ds(first, count)]
        return remote(ref, ref, end_send.at[part, number], end_recv.at[part, number], to)

    def send_sums(part):
        half, first, count = PARTS[part]
        rows, columns = slice(first, first + count), slice(half * HALF, (half + 1) * HALF)
        sent[half, rows] = total_far[rows, columns].astype(jnp.bfloat16)
        sums_copy(part).start()

    def finish(part):
        half, first, count = PARTS[part]
        rows, columns = slice(first, first + count), slice(half * HALF, (half + 1) * HALF)
        sums_copy(part).wait_recv()
        gathered[half, dp, rows] = (
            total[rows, columns] + came[half, rows].astype(jnp.float32)
        ).astype(jnp.bfloat16)
        for name in ("mine_up", "mine_far", "mine_right", "mine_left"):
            gather(part, name).start()
        write(part, 0).start()

    def hand_on(part):
        gather(part, "mine_up").wait_recv()
        gather(part, "twin_right").start()
        gather(part, "twin_left").start()
        gather(part, "mine_far").wait_recv()
        gather(part, "far_up").start()
        write(part, 3).start()
        write(part, 4).start()

    def close(part):
        for number, name in (
            (1, "mine_right"),
            (2, "mine_left"),
            (5, "twin_right"),
            (6, "twin_left"),
            (7, "far_up"),
        ):
            gather(part, name).wait_recv()
            write(part, number).start()

    near_hidden.wait()
    pick_near(0, 0, 6)
    from_across(0)
    pick_near(0, 6, 6)
    from_across(1)
    ring(0)
    from_beside(0)
    near_weights.wait()
    core_copy(0).wait_recv()
    multiply_near(0)
    core_copy(1).wait_recv()
    multiply_near(1)
    from_across(2)
    from_beside(1)
    from_across(3)
    ring(1)
    from_beside(2)
    core_copy(2).wait_recv()
    multiply_near(2)
    meta_copy.wait_recv()
    pick_far(0)
    from_across(4)
    from_beside(3)
    ring(2)
    from_across(5)
    from_across(6)
    core_copy(3).wait_recv()
    multiply_near(3)
    from_beside(4)
    pick_near(1, 0, 6)
    from_beside(5)
    from_beside(6)
    pick_far(1)
    ring(3)
    pick_near(1, 6, 6)
    core_copy(4).wait_recv()
    multiply_near(4)
    pick_far(2)
    multiply_far(0)
    ring(4)
    for group in range(1, 5):
        multiply_far(group)
    core_copy(5).wait_recv()
    multiply_near(5)
    multiply_far(5)
    ring(5)
    core_copy(6).wait_recv()
    multiply_near(6, 0)
    multiply_far(6, 0)
    ring(6)
    core_copy(7).wait_recv()
    multiply_far(7, 0)
    send_sums(0)
    multiply_near(7, 0)
    ring(7)
    core_copy(8).wait_recv()
    multiply_near(6, 1)
    multiply_far(6, 1)
    finish(0)
    ring(8)
    multiply_far(7, 1, 0, 2)
    multiply_near(7, 1, 0, 2)
    core_copy(9).wait_recv()
    multiply_far(7, 1, 2, 2)
    send_sums(1)
    send_sums(2)
    multiply_near(7, 1, 2, 2)
    hand_on(0)
    finish(1)
    finish(2)
    hand_on(1)
    hand_on(2)
    for part in range(len(PARTS)):
        close(part)

    for way in (0, 1):
        for step in range(STEPS):
            ring_copy(way, step).wait_send()
    for number in range(STEPS + 1):
        core_copy(number).wait_send()
    for kind in range(4):
        for sub in range(SUBS):
            rows_copy(kind, sub).wait_send()
    meta_copy.wait_send()
    for part in range(len(PARTS)):
        sums_copy(part).wait_send()
        for name in gathers:
            gather(part, name).wait_send()
        for number in range(len(blocks)):
            write(part, number).wait()


def local(hidden, expert_ids, route_gates, down_weight):
    routes = TOKENS * TOP
    anywhere = pl.BlockSpec(memory_space=pl.ANY)
    dma = pltpu.SemaphoreType.DMA
    return pl.pallas_call(
        kernel,
        out_shape=pltpu.VMEM((TOKENS, 8 * COLS), jnp.bfloat16),
        in_specs=[pl.BlockSpec(memory_space=pltpu.VMEM)] * 2 + [anywhere] * 2,
        out_specs=anywhere,
        scratch_shapes=[
            pltpu.VMEM((2 * BLOCKS, ROUTES), jnp.float32),
            pltpu.VMEM((4 * (WHOLE + 1) * FF, COLS), jnp.bfloat16),
            pltpu.VMEM((2, 4 * LATE * FF, HALF), jnp.bfloat16),
            pltpu.VMEM((routes, FF), jnp.bfloat16),
            pltpu.VMEM((routes, FF), jnp.bfloat16),
            pltpu.VMEM((2 * BLOCKS, ROUTES), jnp.float32),
            pltpu.VMEM((TOKENS, OWN_BATCH * FF), jnp.bfloat16),
            pltpu.VMEM((TOKENS, 32 * FF), jnp.bfloat16),
            pltpu.VMEM((TOKENS, COLS), jnp.float32),
            pltpu.VMEM((TOKENS, COLS), jnp.float32),
            pltpu.VMEM((2, TOKENS, HALF), jnp.bfloat16),
            pltpu.VMEM((2, TOKENS, HALF), jnp.bfloat16),
            pltpu.VMEM((2, 8, TOKENS, HALF), jnp.bfloat16),
            dma((2, STEPS)),
            dma((2, STEPS)),
            dma((STEPS + 1,)),
            dma((STEPS + 1,)),
            dma((4, SUBS)),
            dma((4, SUBS)),
            dma((len(PARTS), 8)),
            dma((len(PARTS), 8)),
            dma((2,)),
            dma((2,)),
            dma((len(PARTS), 8)),
        ],
        name="experts",
        compiler_params=pltpu.CompilerParams(
            collective_id=0, has_side_effects=True, vmem_limit_bytes=60 * 2**20
        ),
        cost_estimate=pl.CostEstimate(
            flops=2 * 2 * TOKENS * 32 * FF * COLS * 2,
            bytes_accessed=8 * 2**20,
            transcendentals=0,
        ),
    )(expert_ids.T, route_gates.T, hidden.reshape(routes, FF), down_weight.reshape(2 * FF, COLS))


def solution(mesh):
    placed = (
        P("expert", None, None),
        P("expert", None),
        P("expert", None),
        P("expert", None, "dp"),
    )
    return jax.shard_map(
        local, mesh=mesh, in_specs=placed, out_specs=P("expert", None), check_vma=False
    )
```

```python
import functools

import jax
import jax.numpy as jnp
from jax import lax
from jax.experimental import pallas as pl
from jax.experimental.pallas import tpu as pltpu
from jax.sharding import PartitionSpec as P

MESH = pl.DeviceIdType.MESH
TOKENS = 384
TOP = 8
FF = 768
COLS = 256
BLOCK = 32
BLOCKS = TOKENS // BLOCK
THREE = 3
ROUTES = BLOCK * TOP
HOPS = 7
QUARTER = TOKENS * TOP // 4
PIECES = (128, 128, 128, 128, 128, 64, 64)
SUBS = len(PIECES)
WHOLE = 5
LATE = HOPS - WHOLE
HALF = COLS // 2
STEPS = WHOLE + 2 * LATE
PARTS = ((0, 0, TOKENS), (1, 0, TOKENS // 2), (1, TOKENS // 2, TOKENS // 2))


def pick_rows(meta, hidden, picked, block, place, experts):
    ids = meta[pl.ds(block, 1), :]
    gates = meta[pl.ds(BLOCKS + block, 1), :]
    shape = (BLOCK, ROUTES)
    owner = lax.broadcasted_iota(jnp.int32, shape, 1) // TOP
    mine = owner == lax.broadcasted_iota(jnp.int32, shape, 0)
    names = jnp.where(mine, jnp.broadcast_to(ids, shape), -1.0)
    chosen = jnp.concatenate(
        [jnp.where(names == e, 1.0, 0.0).astype(jnp.bfloat16) for e in experts], axis=0
    )
    square = (ROUTES, ROUTES)
    diagonal = lax.broadcasted_iota(jnp.int32, square, 0) == lax.broadcasted_iota(
        jnp.int32, square, 1
    )
    column = jnp.sum(
        jnp.where(diagonal, jnp.broadcast_to(gates, square), 0.0), axis=1, keepdims=True
    )
    rows = hidden[pl.ds(pl.multiple_of(place * ROUTES, ROUTES), ROUTES), :]
    rows = (rows.astype(jnp.float32) * column).astype(jnp.bfloat16)
    result = jnp.dot(chosen, rows, preferred_element_type=jnp.float32).astype(jnp.bfloat16)
    for i in range(len(experts)):
        picked[pl.ds(pl.multiple_of(block * BLOCK, BLOCK), BLOCK), i * FF : (i + 1) * FF] = result[
            i * BLOCK : (i + 1) * BLOCK
        ]


def lay_out(ids, gates, meta):
    wide = (128, ROUTES)
    spread = (
        lax.rem(lax.broadcasted_iota(jnp.int32, (TOP, ROUTES), 1), TOP)
        == lax.broadcasted_iota(jnp.int32, (TOP, ROUTES), 0)
    ).astype(jnp.float32)
    mine = lax.broadcasted_iota(jnp.int32, wide, 1) // TOP == lax.rem(
        lax.broadcasted_iota(jnp.int32, wide, 0), BLOCK
    )
    for chunk in range(TOKENS // 128):
        columns = slice(chunk * 128, (chunk + 1) * 128)
        for first, part in ((0, ids[:, columns].astype(jnp.float32)), (BLOCKS, gates[:, columns])):
            full = lax.dot_general(
                part,
                spread,
                (((0,), (0,)), ((), ())),
                precision=lax.Precision.HIGHEST,
                preferred_element_type=jnp.float32,
            )
            full = jnp.where(mine, full, 0.0)
            for i in range(128 // BLOCK):
                row = first + chunk * (128 // BLOCK) + i
                meta[row : row + 1, :] = jnp.sum(
                    full[i * BLOCK : (i + 1) * BLOCK], axis=0, keepdims=True
                )


def kernel(
    ids_in,
    gates_in,
    hidden_in,
    weights_in,
    out,
    meta,
    held,
    late,
    hidden,
    hidden_far,
    meta_far,
    picked,
    picked_far,
    total,
    total_far,
    sent,
    came,
    ring_send,
    ring_recv,
    core_send,
    core_recv,
    rows_send,
    rows_recv,
    end_send,
    end_recv,
    meta_sem,
    near_sem,
):
    dp = lax.axis_index("dp")
    ex = lax.axis_index("expert")
    x, y_lo = lax.rem(dp, 4), dp // 4
    z, y_hi, core = ex // 4, lax.rem(ex // 2, 2), lax.rem(ex, 2)

    def device(x_, y_lo_, z_, y_hi_, core_):
        return (y_lo_ * 4 + lax.rem(x_ + 4, 4), lax.rem(z_ + 8, 8) * 4 + y_hi_ * 2 + core_)

    up, down = device(x, y_lo, z + 1, y_hi, core), device(x, y_lo, z - 1, y_hi, core)
    sibling = device(x, y_lo, z, y_hi, 1 - core)
    across = device(x, 1 - y_lo, z, 1 - y_hi, core)
    beside = device(x, 1 - y_lo, z, y_hi, core)
    right, left = device(x + 1, y_lo, z, y_hi, core), device(x - 1, y_lo, z, y_hi, core)
    opposite = device(x, y_lo, z, 1 - y_hi, core)
    farther = device(x + 2, y_lo, z, y_hi, core)

    def remote(src, dst, send_sem, recv_sem, to):
        return pltpu.make_async_remote_copy(
            src_ref=src,
            dst_ref=dst,
            send_sem=send_sem,
            recv_sem=recv_sem,
            device_id=to,
            device_id_type=MESH,
        )

    def place(group, first, count):
        return held.at[pl.ds((4 * group + first) * FF, count * FF)]

    def late_place(half, group, first, count):
        return late.at[half, pl.ds((4 * (group - WHOLE - 1) + first) * FF, count * FF)]

    def hop_of(step):
        if step < WHOLE:
            return step, None
        return WHOLE + (step - WHOLE) % LATE, (step - WHOLE) // LATE

    def ring_copy(way, step):
        hop, half = hop_of(step)
        if hop < 2:
            src = weights_in.at[pl.ds((hop if way == 0 else 1 - hop) * FF, FF)]
        elif hop - 2 < WHOLE:
            src = place(hop - 1, way, 1)
            if half is not None:
                src = held.at[pl.ds((4 * (hop - 1) + way) * FF, FF), pl.ds(half * HALF, HALF)]
        else:
            src = late_place(half, hop - 1, way, 1)
        dst = place(hop + 1, way, 1) if half is None else late_place(half, hop + 1, way, 1)
        return remote(
            src,
            dst,
            ring_send.at[way, step],
            ring_recv.at[way, step],
            up if way == 0 else down,
        )

    def core_copy(number):
        if number == 0:
            src, dst = weights_in, place(0, 2, 2)
        else:
            hop, half = hop_of(number - 1)
            if half is None:
                src, dst = place(hop + 1, 0, 2), place(hop + 1, 2, 2)
            else:
                src, dst = late_place(half, hop + 1, 0, 2), late_place(half, hop + 1, 2, 2)
        return remote(src, dst, core_send.at[number], core_recv.at[number], sibling)

    def experts_of(group):
        found = []
        for c in (core, 1 - core):
            for way in (0, 1):
                if group == 0:
                    where, which = z, way
                else:
                    hop = group - 1
                    step = 1 + hop // 2
                    where = lax.rem(z + (8 - step if way == 0 else step), 8)
                    which = hop % 2 if way == 0 else 1 - hop % 2
                found.append(((where * 2 + y_hi) * 2 + c) * 2 + which)
        return [e.astype(jnp.float32) for e in found]

    x_odd = lax.rem(x, 2)
    quarters = [
        x_odd * 2 + y_lo,
        x_odd * 2 + 1 - y_lo,
        (1 - x_odd) * 2 + y_lo,
        (1 - x_odd) * 2 + 1 - y_lo,
    ]

    def rows_of(quarter, sub):
        start = pl.multiple_of(quarter * QUARTER + sum(PIECES[:sub]), 64)
        return pl.ds(start, PIECES[sub])

    def rows_copy(kind, sub):
        quarter = quarters[(1, 0, 0, 1)[kind]]
        rows = rows_of(quarter, sub)
        src = (hidden_in if kind == 0 else hidden_far).at[rows]
        to = (across, beside, left, right)[kind]
        return remote(
            src, hidden_far.at[rows], rows_send.at[kind, sub], rows_recv.at[kind, sub], to
        )

    meta_copy = remote(meta, meta_far, meta_sem.at[0], meta_sem.at[1], across)

    barrier = pltpu.get_barrier_semaphore()
    friends = (up, down, sibling, across, beside, right, left, opposite, farther)
    for friend in friends:
        pl.semaphore_signal(barrier, inc=1, device_id=friend, device_id_type=MESH)
    def near_hidden(turn):
        count = THREE * ROUTES
        return pltpu.make_async_copy(
            hidden_in.at[pl.ds(turn * count, count)],
            hidden.at[pl.ds(turn % 2 * count, count)],
            near_sem.at[1 + turn],
        )

    near_weights = pltpu.make_async_copy(weights_in, place(0, 0, 2), near_sem.at[0])
    near_hidden(0).start()
    near_hidden(1).start()
    near_weights.start()
    pl.semaphore_wait(barrier, len(friends))

    for hop in (0, 1):
        for way in (0, 1):
            ring_copy(way, hop).start()
    for sub in range(SUBS):
        rows_copy(0, sub).start()
    core_copy(0).start()
    lay_out(ids_in, gates_in, meta)
    meta_copy.start()

    total[...] = jnp.zeros_like(total)
    total_far[...] = jnp.zeros_like(total_far)
    experts = [e for group in range(8) for e in experts_of(group)]

    def ring(step):
        for way in (0, 1):
            ring_copy(way, step).wait_recv()
            if step + 2 < STEPS:
                ring_copy(way, step + 2).start()
        core_copy(step + 1).start()

    def from_across(sub):
        rows_copy(0, sub).wait_recv()
        rows_copy(1, sub).start()
        rows_copy(2, sub).start()

    def from_beside(sub):
        rows_copy(1, sub).wait_recv()
        rows_copy(3, sub).start()

    def pick_near(turn):
        near_hidden(turn).wait()

        @pl.loop(0, THREE)
        def _(i):
            pick_rows(meta, hidden, picked, turn * THREE + i, turn % 2 * THREE + i, experts)

        if turn + 2 < BLOCKS // THREE:
            near_hidden(turn + 2).start()

    def pick_far(turn, pair):
        if pair == 1:
            for kind in (2, 3):
                for sub in range(2 * turn, 2 * turn + 2 + turn // 2):
                    rows_copy(kind, sub).wait_recv()
        odd = x_odd if pair == 0 else 1 - x_odd

        @pl.loop(0, 2)
        def _(i):
            low = y_lo + i * (1 - 2 * y_lo)
            block = (odd * 2 + low) * (BLOCKS // 4) + turn
            pick_rows(meta_far, hidden_far, picked_far, block, block, experts)

    def multiply(acc, rows, group, half, first=0, count=4):
        left = rows[:, (group * 4 + first) * FF : (group * 4 + first + count) * FF]
        if half is None:
            start = (group * 4 + first) * FF
            acc[...] += jnp.dot(
                left, held[start : start + count * FF, :], preferred_element_type=jnp.float32
            )
        else:
            start = ((group - WHOLE - 1) * 4 + first) * FF
            acc[:, half * HALF : (half + 1) * HALF] += jnp.dot(
                left, late[half, start : start + count * FF, :], preferred_element_type=jnp.float32
            )

    def multiply_near(group, half=None, first=0, count=4):
        multiply(total, picked, group, half, first, count)

    def multiply_far(group, half=None, first=0, count=4):
        multiply(total_far, picked_far, group, half, first, count)

    dp_of = lambda x_, y_lo_: y_lo_ * 4 + lax.rem(x_ + 4, 4)
    far, twin = dp_of(x + 2, y_lo), dp_of(x, 1 - y_lo)

    def columns_of(block, half):
        return pl.ds(pl.multiple_of(block * COLS + half * HALF, HALF), HALF)

    def sums_copy(part):
        half, first, count = PARTS[part]
        rows = pl.ds(first, count)
        return remote(
            sent.at[half, rows],
            came.at[half, rows],
            end_send.at[part, 0],
            end_recv.at[part, 0],
            opposite,
        )

    gathers = {
        "mine_up": (1, dp, beside),
        "mine_far": (2, dp, farther),
        "mine_right": (3, dp, right),
        "mine_left": (4, dp, left),
        "twin_right": (5, twin, right),
        "twin_left": (6, twin, left),
        "far_up": (7, far, beside),
    }

    def gather(part, name):
        half, first, count = PARTS[part]
        number, block, to = gathers[name]
        ref = out.at[pl.ds(first, count), columns_of(block, half)]
        return remote(ref, ref, end_send.at[part, number], end_recv.at[part, number], to)

    def send_sums(part):
        half, first, count = PARTS[part]
        rows, columns = slice(first, first + count), slice(half * HALF, (half + 1) * HALF)
        sent[half, rows] = total_far[rows, columns].astype(jnp.bfloat16)
        sums_copy(part).start()

    def finish(part):
        half, first, count = PARTS[part]
        rows, columns = slice(first, first + count), slice(half * HALF, (half + 1) * HALF)
        sums_copy(part).wait_recv()
        out[rows, columns_of(dp, half)] = (
            total[rows, columns] + came[half, rows].astype(jnp.float32)
        ).astype(jnp.bfloat16)
        for name in ("mine_up", "mine_far", "mine_right", "mine_left"):
            gather(part, name).start()

    def hand_on(part):
        gather(part, "mine_up").wait_recv()
        gather(part, "twin_right").start()
        gather(part, "twin_left").start()
        gather(part, "mine_far").wait_recv()
        gather(part, "far_up").start()

    def close(part):
        for name in ("mine_right", "mine_left", "twin_right", "twin_left", "far_up"):
            gather(part, name).wait_recv()

    pick_near(0)
    pick_near(1)
    from_across(0)
    pick_near(2)
    from_across(1)
    ring(0)
    from_beside(0)
    pick_near(3)
    near_weights.wait()
    core_copy(0).wait_recv()
    multiply_near(0)
    from_across(2)
    from_beside(1)
    meta_copy.wait_recv()
    pick_far(0, 0)
    from_across(3)
    ring(1)
    from_beside(2)
    core_copy(1).wait_recv()
    multiply_near(1)
    pick_far(0, 1)
    from_across(4)
    from_beside(3)
    pick_far(1, 0)
    ring(2)
    from_across(5)
    from_across(6)
    from_beside(4)
    core_copy(2).wait_recv()
    multiply_near(2)
    pick_far(1, 1)
    from_beside(5)
    from_beside(6)
    pick_far(2, 0)
    core_copy(3).wait_recv()
    multiply_near(3)
    ring(3)
    pick_far(2, 1)
    multiply_far(0)
    multiply_far(1)
    ring(4)
    multiply_far(2)
    multiply_far(3)
    core_copy(4).wait_recv()
    multiply_near(4)
    multiply_far(4)
    ring(5)
    core_copy(5).wait_recv()
    multiply_near(5)
    multiply_far(5)
    core_copy(6).wait_recv()
    multiply_near(6, 0)
    multiply_far(6, 0)
    ring(6)
    core_copy(7).wait_recv()
    multiply_far(7, 0)
    send_sums(0)
    multiply_near(7, 0)
    ring(7)
    core_copy(8).wait_recv()
    multiply_near(6, 1)
    multiply_far(6, 1)
    finish(0)
    ring(8)
    multiply_far(7, 1, 0, 2)
    multiply_near(7, 1, 0, 2)
    core_copy(9).wait_recv()
    multiply_far(7, 1, 2, 2)
    send_sums(1)
    send_sums(2)
    hand_on(0)
    multiply_near(7, 1, 2, 2)
    finish(1)
    finish(2)
    hand_on(1)
    hand_on(2)
    for part in range(len(PARTS)):
        close(part)

    for way in (0, 1):
        for step in range(STEPS):
            ring_copy(way, step).wait_send()
    for number in range(STEPS + 1):
        core_copy(number).wait_send()
    for kind in range(4):
        for sub in range(SUBS):
            rows_copy(kind, sub).wait_send()
    meta_copy.wait_send()
    for part in range(len(PARTS)):
        sums_copy(part).wait_send()
        for name in gathers:
            gather(part, name).wait_send()


def local(hidden, expert_ids, route_gates, down_weight):
    routes = TOKENS * TOP
    anywhere = pl.BlockSpec(memory_space=pl.ANY)
    dma = pltpu.SemaphoreType.DMA
    return pl.pallas_call(
        kernel,
        out_shape=pltpu.VMEM((TOKENS, 8 * COLS), jnp.bfloat16),
        in_specs=[pl.BlockSpec(memory_space=pltpu.VMEM)] * 2 + [anywhere] * 2,
        out_specs=pl.BlockSpec(memory_space=pltpu.VMEM),
        scratch_shapes=[
            pltpu.VMEM((2 * BLOCKS, ROUTES), jnp.float32),
            pltpu.VMEM((4 * (WHOLE + 1) * FF, COLS), jnp.bfloat16),
            pltpu.VMEM((2, 4 * LATE * FF, HALF), jnp.bfloat16),
            pltpu.VMEM((2 * THREE * ROUTES, FF), jnp.bfloat16),
            pltpu.VMEM((routes, FF), jnp.bfloat16),
            pltpu.VMEM((2 * BLOCKS, ROUTES), jnp.float32),
            pltpu.VMEM((TOKENS, 32 * FF), jnp.bfloat16),
            pltpu.VMEM((TOKENS, 32 * FF), jnp.bfloat16),
            pltpu.VMEM((TOKENS, COLS), jnp.float32),
            pltpu.VMEM((TOKENS, COLS), jnp.float32),
            pltpu.VMEM((2, TOKENS, HALF), jnp.bfloat16),
            pltpu.VMEM((2, TOKENS, HALF), jnp.bfloat16),
            dma((2, STEPS)),
            dma((2, STEPS)),
            dma((STEPS + 1,)),
            dma((STEPS + 1,)),
            dma((4, SUBS)),
            dma((4, SUBS)),
            dma((len(PARTS), 8)),
            dma((len(PARTS), 8)),
            dma((2,)),
            dma((1 + BLOCKS // THREE,)),
        ],
        name="experts",
        compiler_params=pltpu.CompilerParams(
            collective_id=0, has_side_effects=True, vmem_limit_bytes=61 * 2**20
        ),
        cost_estimate=pl.CostEstimate(
            flops=2 * 2 * TOKENS * 32 * FF * COLS * 2,
            bytes_accessed=8 * 2**20,
            transcendentals=0,
        ),
    )(expert_ids.T, route_gates.T, hidden.reshape(routes, FF), down_weight.reshape(2 * FF, COLS))


def solution(mesh):
    placed = (
        P("expert", None, None),
        P("expert", None),
        P("expert", None),
        P("expert", None, "dp"),
    )
    return jax.shard_map(
        local, mesh=mesh, in_specs=placed, out_specs=P("expert", None), check_vma=False
    )
```

```python
import functools

import jax
import jax.numpy as jnp
from jax import lax
from jax.experimental import pallas as pl
from jax.experimental.pallas import tpu as pltpu
from jax.sharding import PartitionSpec as P

MESH = pl.DeviceIdType.MESH
TOKENS = 384
TOP = 8
FF = 768
COLS = 256
BLOCK = 32
BLOCKS = TOKENS // BLOCK
THREE = 3
ROUTES = BLOCK * TOP
HOPS = 7
QUARTER = TOKENS * TOP // 4
PIECES = (128, 128, 128, 128, 128, 64, 64)
SUBS = len(PIECES)
WHOLE = 6
LATE = HOPS - WHOLE
HALF = COLS // 2
STEPS = WHOLE + 2 * LATE
PARTS = ((0, 0, TOKENS), (1, 0, TOKENS // 2), (1, TOKENS // 2, TOKENS // 2))


def pick_rows(meta, hidden, picked, block, place, experts):
    ids = meta[pl.ds(block, 1), :]
    gates = meta[pl.ds(BLOCKS + block, 1), :]
    shape = (BLOCK, ROUTES)
    owner = lax.broadcasted_iota(jnp.int32, shape, 1) // TOP
    mine = owner == lax.broadcasted_iota(jnp.int32, shape, 0)
    names = jnp.where(mine, jnp.broadcast_to(ids, shape), -1.0)
    chosen = jnp.concatenate(
        [jnp.where(names == e, 1.0, 0.0).astype(jnp.bfloat16) for e in experts], axis=0
    )
    square = (ROUTES, ROUTES)
    diagonal = lax.broadcasted_iota(jnp.int32, square, 0) == lax.broadcasted_iota(
        jnp.int32, square, 1
    )
    column = jnp.sum(
        jnp.where(diagonal, jnp.broadcast_to(gates, square), 0.0), axis=1, keepdims=True
    )
    rows = hidden[pl.ds(pl.multiple_of(place * ROUTES, ROUTES), ROUTES), :]
    rows = (rows.astype(jnp.float32) * column).astype(jnp.bfloat16)
    result = jnp.dot(chosen, rows, preferred_element_type=jnp.float32).astype(jnp.bfloat16)
    for i in range(len(experts)):
        picked[pl.ds(pl.multiple_of(block * BLOCK, BLOCK), BLOCK), i * FF : (i + 1) * FF] = result[
            i * BLOCK : (i + 1) * BLOCK
        ]


def lay_out(ids, gates, meta):
    wide = (128, ROUTES)
    spread = (
        lax.rem(lax.broadcasted_iota(jnp.int32, (TOP, ROUTES), 1), TOP)
        == lax.broadcasted_iota(jnp.int32, (TOP, ROUTES), 0)
    ).astype(jnp.float32)
    mine = lax.broadcasted_iota(jnp.int32, wide, 1) // TOP == lax.rem(
        lax.broadcasted_iota(jnp.int32, wide, 0), BLOCK
    )
    for chunk in range(TOKENS // 128):
        columns = slice(chunk * 128, (chunk + 1) * 128)
        for first, part in ((0, ids[:, columns].astype(jnp.float32)), (BLOCKS, gates[:, columns])):
            full = lax.dot_general(
                part,
                spread,
                (((0,), (0,)), ((), ())),
                precision=lax.Precision.HIGHEST,
                preferred_element_type=jnp.float32,
            )
            full = jnp.where(mine, full, 0.0)
            for i in range(128 // BLOCK):
                row = first + chunk * (128 // BLOCK) + i
                meta[row : row + 1, :] = jnp.sum(
                    full[i * BLOCK : (i + 1) * BLOCK], axis=0, keepdims=True
                )


def kernel(
    ids_in,
    gates_in,
    hidden_in,
    weights_in,
    out,
    meta,
    held,
    late,
    hidden,
    hidden_far,
    meta_far,
    picked,
    picked_far,
    total,
    total_far,
    sent,
    came,
    ring_send,
    ring_recv,
    core_send,
    core_recv,
    rows_send,
    rows_recv,
    end_send,
    end_recv,
    meta_sem,
    near_sem,
):
    dp = lax.axis_index("dp")
    ex = lax.axis_index("expert")
    x, y_lo = lax.rem(dp, 4), dp // 4
    z, y_hi, core = ex // 4, lax.rem(ex // 2, 2), lax.rem(ex, 2)

    def device(x_, y_lo_, z_, y_hi_, core_):
        return (y_lo_ * 4 + lax.rem(x_ + 4, 4), lax.rem(z_ + 8, 8) * 4 + y_hi_ * 2 + core_)

    up, down = device(x, y_lo, z + 1, y_hi, core), device(x, y_lo, z - 1, y_hi, core)
    sibling = device(x, y_lo, z, y_hi, 1 - core)
    across = device(x, 1 - y_lo, z, 1 - y_hi, core)
    beside = device(x, 1 - y_lo, z, y_hi, core)
    right, left = device(x + 1, y_lo, z, y_hi, core), device(x - 1, y_lo, z, y_hi, core)
    opposite = device(x, y_lo, z, 1 - y_hi, core)
    farther = device(x + 2, y_lo, z, y_hi, core)

    def remote(src, dst, send_sem, recv_sem, to):
        return pltpu.make_async_remote_copy(
            src_ref=src,
            dst_ref=dst,
            send_sem=send_sem,
            recv_sem=recv_sem,
            device_id=to,
            device_id_type=MESH,
        )

    def place(group, first, count):
        return held.at[pl.ds((4 * group + first) * FF, count * FF)]

    def late_place(half, group, first, count):
        return late.at[half, pl.ds((4 * (group - WHOLE - 1) + first) * FF, count * FF)]

    def hop_of(step):
        if step < WHOLE:
            return step, None
        return WHOLE + (step - WHOLE) % LATE, (step - WHOLE) // LATE

    def ring_copy(way, step):
        hop, half = hop_of(step)
        if hop < 2:
            src = weights_in.at[pl.ds((hop if way == 0 else 1 - hop) * FF, FF)]
        elif hop - 2 < WHOLE:
            src = place(hop - 1, way, 1)
            if half is not None:
                src = held.at[pl.ds((4 * (hop - 1) + way) * FF, FF), pl.ds(half * HALF, HALF)]
        else:
            src = late_place(half, hop - 1, way, 1)
        dst = place(hop + 1, way, 1) if half is None else late_place(half, hop + 1, way, 1)
        return remote(
            src,
            dst,
            ring_send.at[way, step],
            ring_recv.at[way, step],
            up if way == 0 else down,
        )

    def core_copy(number):
        if number == 0:
            src, dst = weights_in, place(0, 2, 2)
        else:
            hop, half = hop_of(number - 1)
            if half is None:
                src, dst = place(hop + 1, 0, 2), place(hop + 1, 2, 2)
            else:
                src, dst = late_place(half, hop + 1, 0, 2), late_place(half, hop + 1, 2, 2)
        return remote(src, dst, core_send.at[number], core_recv.at[number], sibling)

    def experts_of(group):
        found = []
        for c in (core, 1 - core):
            for way in (0, 1):
                if group == 0:
                    where, which = z, way
                else:
                    hop = group - 1
                    step = 1 + hop // 2
                    where = lax.rem(z + (8 - step if way == 0 else step), 8)
                    which = hop % 2 if way == 0 else 1 - hop % 2
                found.append(((where * 2 + y_hi) * 2 + c) * 2 + which)
        return [e.astype(jnp.float32) for e in found]

    x_odd = lax.rem(x, 2)
    quarters = [
        x_odd * 2 + y_lo,
        x_odd * 2 + 1 - y_lo,
        (1 - x_odd) * 2 + y_lo,
        (1 - x_odd) * 2 + 1 - y_lo,
    ]

    def rows_of(quarter, sub):
        start = pl.multiple_of(quarter * QUARTER + sum(PIECES[:sub]), 64)
        return pl.ds(start, PIECES[sub])

    def rows_copy(kind, sub):
        quarter = quarters[(1, 0, 0, 1)[kind]]
        rows = rows_of(quarter, sub)
        src = (hidden_in if kind == 0 else hidden_far).at[rows]
        to = (across, beside, left, right)[kind]
        return remote(
            src, hidden_far.at[rows], rows_send.at[kind, sub], rows_recv.at[kind, sub], to
        )

    meta_copy = remote(meta, meta_far, meta_sem.at[0], meta_sem.at[1], across)

    barrier = pltpu.get_barrier_semaphore()
    friends = (up, down, sibling, across, beside, right, left, opposite, farther)
    for friend in friends:
        pl.semaphore_signal(barrier, inc=1, device_id=friend, device_id_type=MESH)
    def near_hidden(turn):
        count = THREE * ROUTES
        return pltpu.make_async_copy(
            hidden_in.at[pl.ds(turn * count, count)],
            hidden.at[pl.ds(turn % 2 * count, count)],
            near_sem.at[1 + turn],
        )

    near_weights = pltpu.make_async_copy(weights_in, place(0, 0, 2), near_sem.at[0])
    near_hidden(0).start()
    near_hidden(1).start()
    near_weights.start()
    pl.semaphore_wait(barrier, len(friends))

    for hop in (0, 1):
        for way in (0, 1):
            ring_copy(way, hop).start()
    for sub in range(SUBS):
        rows_copy(0, sub).start()
    core_copy(0).start()
    lay_out(ids_in, gates_in, meta)
    meta_copy.start()

    total[...] = jnp.zeros_like(total)
    total_far[...] = jnp.zeros_like(total_far)
    experts = [e for group in range(8) for e in experts_of(group)]

    def ring(step):
        following = (step + 2,) if step + 2 < WHOLE else ()
        if step == WHOLE - 2:
            following = range(WHOLE, STEPS)
        for way in (0, 1):
            ring_copy(way, step).wait_recv()
            for later in following:
                ring_copy(way, later).start()
        core_copy(step + 1).start()

    def from_across(sub):
        rows_copy(0, sub).wait_recv()
        rows_copy(1, sub).start()
        rows_copy(2, sub).start()

    def from_beside(sub):
        rows_copy(1, sub).wait_recv()
        rows_copy(3, sub).start()

    def pick_near(turn):
        near_hidden(turn).wait()

        @pl.loop(0, THREE)
        def _(i):
            pick_rows(meta, hidden, picked, turn * THREE + i, turn % 2 * THREE + i, experts)

        if turn + 2 < BLOCKS // THREE:
            near_hidden(turn + 2).start()

    def pick_far(turn, pair):
        if pair == 1:
            for kind in (2, 3):
                for sub in range(2 * turn, 2 * turn + 2 + turn // 2):
                    rows_copy(kind, sub).wait_recv()
        odd = x_odd if pair == 0 else 1 - x_odd

        @pl.loop(0, 2)
        def _(i):
            low = y_lo + i * (1 - 2 * y_lo)
            block = (odd * 2 + low) * (BLOCKS // 4) + turn
            pick_rows(meta_far, hidden_far, picked_far, block, block, experts)

    def multiply(acc, rows, group, half, first=0, count=4):
        left = rows[:, (group * 4 + first) * FF : (group * 4 + first + count) * FF]
        if half is None:
            start = (group * 4 + first) * FF
            acc[...] += jnp.dot(
                left, held[start : start + count * FF, :], preferred_element_type=jnp.float32
            )
        else:
            start = ((group - WHOLE - 1) * 4 + first) * FF
            acc[:, half * HALF : (half + 1) * HALF] += jnp.dot(
                left, late[half, start : start + count * FF, :], preferred_element_type=jnp.float32
            )

    def multiply_near(group, half=None, first=0, count=4):
        multiply(total, picked, group, half, first, count)

    def multiply_far(group, half=None, first=0, count=4):
        multiply(total_far, picked_far, group, half, first, count)

    dp_of = lambda x_, y_lo_: y_lo_ * 4 + lax.rem(x_ + 4, 4)
    far, twin = dp_of(x + 2, y_lo), dp_of(x, 1 - y_lo)

    def columns_of(block, half):
        return pl.ds(pl.multiple_of(block * COLS + half * HALF, HALF), HALF)

    def sums_copy(part):
        half, first, count = PARTS[part]
        rows = pl.ds(first, count)
        return remote(
            sent.at[half, rows],
            came.at[half, rows],
            end_send.at[part, 0],
            end_recv.at[part, 0],
            opposite,
        )

    gathers = {
        "mine_up": (1, dp, beside),
        "mine_far": (2, dp, farther),
        "mine_right": (3, dp, right),
        "mine_left": (4, dp, left),
        "twin_right": (5, twin, right),
        "twin_left": (6, twin, left),
        "far_up": (7, far, beside),
    }

    def gather(part, name):
        half, first, count = PARTS[part]
        number, block, to = gathers[name]
        ref = out.at[pl.ds(first, count), columns_of(block, half)]
        return remote(ref, ref, end_send.at[part, number], end_recv.at[part, number], to)

    def send_sums(part):
        half, first, count = PARTS[part]
        rows, columns = slice(first, first + count), slice(half * HALF, (half + 1) * HALF)
        sent[half, rows] = total_far[rows, columns].astype(jnp.bfloat16)
        sums_copy(part).start()

    def finish(part):
        half, first, count = PARTS[part]
        rows, columns = slice(first, first + count), slice(half * HALF, (half + 1) * HALF)
        sums_copy(part).wait_recv()
        out[rows, columns_of(dp, half)] = (
            total[rows, columns] + came[half, rows].astype(jnp.float32)
        ).astype(jnp.bfloat16)
        for name in ("mine_up", "mine_far", "mine_right", "mine_left"):
            gather(part, name).start()

    def hand_on(part):
        gather(part, "mine_up").wait_recv()
        gather(part, "twin_right").start()
        gather(part, "twin_left").start()
        gather(part, "mine_far").wait_recv()
        gather(part, "far_up").start()

    def close(part):
        for name in ("mine_right", "mine_left", "twin_right", "twin_left", "far_up"):
            gather(part, name).wait_recv()

    pick_near(0)
    pick_near(1)
    from_across(0)
    pick_near(2)
    from_across(1)
    ring(0)
    from_beside(0)
    pick_near(3)
    near_weights.wait()
    core_copy(0).wait_recv()
    multiply_near(0)
    from_across(2)
    from_beside(1)
    meta_copy.wait_recv()
    pick_far(0, 0)
    from_across(3)
    ring(1)
    from_beside(2)
    core_copy(1).wait_recv()
    multiply_near(1)
    pick_far(0, 1)
    from_across(4)
    from_beside(3)
    pick_far(1, 0)
    ring(2)
    from_across(5)
    from_across(6)
    from_beside(4)
    core_copy(2).wait_recv()
    multiply_near(2)
    pick_far(1, 1)
    from_beside(5)
    from_beside(6)
    pick_far(2, 0)
    core_copy(3).wait_recv()
    multiply_near(3)
    ring(3)
    pick_far(2, 1)
    multiply_far(0)
    multiply_far(1)
    ring(4)
    multiply_far(2)
    multiply_far(3)
    core_copy(4).wait_recv()
    multiply_near(4)
    multiply_far(4)
    ring(5)
    core_copy(5).wait_recv()
    multiply_near(5)
    multiply_far(5)
    core_copy(6).wait_recv()
    multiply_near(6)
    multiply_far(6)
    ring(6)
    core_copy(7).wait_recv()
    multiply_far(7, 0)
    send_sums(0)
    ring(7)
    multiply_near(7, 0)
    multiply_far(7, 1, 0, 2)
    multiply_near(7, 1, 0, 2)
    core_copy(8).wait_recv()
    multiply_far(7, 1, 2, 2)
    send_sums(1)
    send_sums(2)
    finish(0)
    multiply_near(7, 1, 2, 2)
    finish(1)
    finish(2)
    hand_on(0)
    hand_on(1)
    hand_on(2)
    for part in range(len(PARTS)):
        close(part)

    for way in (0, 1):
        for step in range(STEPS):
            ring_copy(way, step).wait_send()
    for number in range(STEPS + 1):
        core_copy(number).wait_send()
    for kind in range(4):
        for sub in range(SUBS):
            rows_copy(kind, sub).wait_send()
    meta_copy.wait_send()
    for part in range(len(PARTS)):
        sums_copy(part).wait_send()
        for name in gathers:
            gather(part, name).wait_send()


def local(hidden, expert_ids, route_gates, down_weight):
    routes = TOKENS * TOP
    anywhere = pl.BlockSpec(memory_space=pl.ANY)
    dma = pltpu.SemaphoreType.DMA
    return pl.pallas_call(
        kernel,
        out_shape=pltpu.VMEM((TOKENS, 8 * COLS), jnp.bfloat16),
        in_specs=[pl.BlockSpec(memory_space=pltpu.VMEM)] * 2 + [anywhere] * 2,
        out_specs=pl.BlockSpec(memory_space=pltpu.VMEM),
        scratch_shapes=[
            pltpu.VMEM((2 * BLOCKS, ROUTES), jnp.float32),
            pltpu.VMEM((4 * (WHOLE + 1) * FF, COLS), jnp.bfloat16),
            pltpu.VMEM((2, 4 * LATE * FF, HALF), jnp.bfloat16),
            pltpu.VMEM((2 * THREE * ROUTES, FF), jnp.bfloat16),
            pltpu.VMEM((routes, FF), jnp.bfloat16),
            pltpu.VMEM((2 * BLOCKS, ROUTES), jnp.float32),
            pltpu.VMEM((TOKENS, 32 * FF), jnp.bfloat16),
            pltpu.VMEM((TOKENS, 32 * FF), jnp.bfloat16),
            pltpu.VMEM((TOKENS, COLS), jnp.float32),
            pltpu.VMEM((TOKENS, COLS), jnp.float32),
            pltpu.VMEM((2, TOKENS, HALF), jnp.bfloat16),
            pltpu.VMEM((2, TOKENS, HALF), jnp.bfloat16),
            dma((2, STEPS)),
            dma((2, STEPS)),
            dma((STEPS + 1,)),
            dma((STEPS + 1,)),
            dma((4, SUBS)),
            dma((4, SUBS)),
            dma((len(PARTS), 8)),
            dma((len(PARTS), 8)),
            dma((2,)),
            dma((1 + BLOCKS // THREE,)),
        ],
        name="experts",
        compiler_params=pltpu.CompilerParams(
            collective_id=0, has_side_effects=True, vmem_limit_bytes=61 * 2**20
        ),
        cost_estimate=pl.CostEstimate(
            flops=2 * 2 * TOKENS * 32 * FF * COLS * 2,
            bytes_accessed=8 * 2**20,
            transcendentals=0,
        ),
    )(expert_ids.T, route_gates.T, hidden.reshape(routes, FF), down_weight.reshape(2 * FF, COLS))


def solution(mesh):
    placed = (
        P("expert", None, None),
        P("expert", None),
        P("expert", None),
        P("expert", None, "dp"),
    )
    return jax.shard_map(
        local, mesh=mesh, in_specs=placed, out_specs=P("expert", None), check_vma=False
    )
```
